32 devices in a mesh: req: 16 (over z, x, core), tp: 2 (over y).
Axes of the slice: x: 2, y: 2, z: 4, core: 2. Of those that a mesh axis runs over, the one named last changes fastest.
Arguments:
- queries: bfloat16 [4096, 7168], P('req', 'tp'), may hold values from -200 to 200
- key_value: bfloat16 [2, 4096, 1024], P(None, 'req', 'tp'), may hold values from -8 to 8
- segment: int32 [4096], P('req'), may hold values from 0 to 7, never falling along the last dimension, each value on 1 to 1024 neighbouring positions
- residual: bfloat16 [4096, 7168], P('req', 'tp'), may hold values from -4 to 4
- out_weight: bfloat16 [7168, 7168], P('tp', 'req'), may hold values from -0.0625 to 0.0625
- head_gain: bfloat16 [7168], P('tp'), may hold values from 0.099609375 to 1.8984375
- vocab_weight: bfloat16 [7168, 64000], P('tp', 'req'), may hold values from -0.21875 to 0.21875
Outputs:
- hidden: bfloat16 [4096, 7168], P('req', 'tp')
- key_cache: bfloat16 [4096, 1024], P('req', 'tp')
- last_norm: float32 [8], replicated
- top_logit: float32 [8], replicated
The draws below stay inside these ranges and needn't reach their ends.
Inputs may be any that keep to these rules, and one draw needn't show every extreme that they name: `segment`: ids never fall; each of the 8 requests has 1 to 1024 tokens, one has exactly 1024.
All inputs are finite; a program needn't handle non-finite values.
Results may differ from the reference program's by a relative error of at most 0.013.
Values may be sent and summed in bfloat16 or wider, within the bound.
A program may use at most 192 MiB of HBM per device.

```python
import math
import jax
import jax.numpy as jnp
import numpy as np
from jax import lax

D = 7168
HD = 128
KVH = 8
GROUP = 7
V = 64000
TOK_DEV = 256
QH = 56
TOKENS = 4096
LMAX = 1024
REQS = 8
N_TP = 2


def base_draw(key, salt, shape):
    return jnp.clip(jax.random.normal(jax.random.fold_in(key, salt), shape, jnp.float32), -6.0, 6.0)


def pair_keys(key):
    base = base_draw(key, 21, (TOKENS, KVH, HD))
    return base


def draw_key_value(key, part):
    keys_part = pair_keys(key).reshape(TOKENS, KVH * HD)
    values_part = base_draw(key, 23, (TOKENS, KVH * HD))
    return jnp.stack([keys_part, values_part]).astype(jnp.bfloat16)


def draw_queries(key, part):
    base = base_draw(key, 24, (TOKENS, KVH, GROUP, HD))
    return base.reshape(TOKENS, QH * HD).astype(jnp.bfloat16)


def steps_of(rng, dims, shards, least, top_value):
    loudness, own = 1.0, jax.random.fold_in(rng, 6)
    for axis_at, shards_of in shards:
        draws = jnp.exp(jax.random.uniform(jax.random.fold_in(own, axis_at), (shards_of,), jnp.float32, least / len(shards), top_value / len(shards)))
        loudness = loudness * jnp.repeat(draws, dims[axis_at] // shards_of).reshape([-1 if axis == axis_at else 1 for axis in range(len(dims))])
    return loudness


def profile(count, total, most, lean):
    weights = [(1 << 20) // math.isqrt(standing ** lean) + 1 for standing in range(2, count + 1)]
    surplus, given = total - most - (count - 1), [1] * (count - 1)
    while surplus > 0:
        movable = [i for i in range(count - 1) if given[i] < most]
        whole, remaining = sum([weights[i] for i in movable]), surplus
        for i in movable:
            extra = min(most - given[i], max(1, remaining * weights[i] // whole), surplus)
            given[i] = given[i] + extra
            surplus = surplus - extra
    return np.array([most] + given)


def uneven_parts(rng, amount, total, reach, lean):
    if amount == 2:
        one = jax.random.randint(rng, (), max(1, total - reach), min(reach, total - 1) + 1)
        return jnp.stack([one, total - one])
    sizes = jnp.asarray(profile(amount, total, reach, lean), jnp.int32)
    twos = (amount - 1) // 2
    donor, taker = sizes[1:1 + 2 * twos:2], sizes[2:2 + 2 * twos:2]
    margin = jnp.minimum(donor - 1, reach - taker)
    passed = jax.random.randint(jax.random.fold_in(rng, 1), (twos,), 0, 1 << 20) % (margin + 1)
    sizes = sizes.at[1:1 + 2 * twos:2].set(donor - passed).at[2:2 + 2 * twos:2].set(taker + passed)
    return sizes[jax.random.permutation(jax.random.fold_in(rng, 2), amount)]


def normal_values(own_key, extent, scale, most, split=(), held_as=jnp.bfloat16):
    entries = jax.random.normal(own_key, extent, jnp.float32) * scale
    if len(split) > 0:
        entries = steps_of(own_key, extent, split, -0.22, 0.18) * entries
    return jnp.clip(entries, min=-most, max=most).astype(held_as)


def setup_inputs(seed: int = 0) -> dict:
    arg_keys = jax.random.split(jax.random.key(seed), 8)
    queries = draw_queries(jax.random.fold_in(arg_keys[7], 71), 0)
    key_value = draw_key_value(jax.random.fold_in(arg_keys[7], 71), 0)
    segment = jnp.searchsorted(jnp.cumsum(uneven_parts(arg_keys[2], REQS, TOKENS, LMAX, 2)), jnp.arange(TOKENS), side="right").astype(jnp.int32)
    residual = normal_values(arg_keys[3], (TOKENS, D), 0.3, 4.0, ((0, 16), (1, 2)))
    out_weight = normal_values(arg_keys[4], (QH * HD, D), (QH * HD) ** -0.5, 0.0625, ((0, 2), (1, 16)))
    head_gain = jnp.clip(1.0 + 0.18 * jax.random.normal(arg_keys[5], (D,), jnp.float32), 0.099609375, 1.8984375).astype(jnp.bfloat16)
    vocab_weight = normal_values(arg_keys[6], (D, V), (D // 9) ** -0.5, 0.21875, ((0, 2), (1, 16)))
    return {"queries": queries, "key_value": key_value, "segment": segment, "residual": residual, "out_weight": out_weight, "head_gain": head_gain, "vocab_weight": vocab_weight}


theta = 5000000.0
eps = 1e-05
masked_score = -1e+30

def rope_tables(positions, width):
    half_width = width // 2
    frequency = theta ** (-(jnp.arange(half_width, dtype=jnp.float32) * 2.0 / width))
    angles = positions[:, None] * frequency[None, :]
    return (jnp.cos(angles), jnp.sin(angles))

def rotate(values, cosine, sine_table):
    half_width = values.shape[-1] // 2
    first_half = values[..., :half_width]
    second_half = values[..., half_width:]
    table_shape = (cosine.shape[0],) + (1,) * (values.ndim - 2) + (half_width,)
    cosine = cosine.reshape(table_shape)
    sine_table = sine_table.reshape(table_shape)
    return jnp.concatenate([first_half * cosine - second_half * sine_table, second_half * cosine + first_half * sine_table], axis=-1)

def reference(queries, key_value, segment, residual, out_weight, head_gain, vocab_weight):
    request_ids = jnp.arange(REQS, dtype=jnp.int32)
    member = segment[:, None] == request_ids[None, :]
    lengths = lax.optimization_barrier(jnp.sum(member.astype(jnp.float32), axis=0))
    starts = jnp.cumsum(lengths) - lengths
    tok_index = jnp.arange(TOKENS, dtype=jnp.int32).astype(jnp.float32)
    own_start = lax.optimization_barrier(jnp.sum(jnp.where(member, starts[None, :], 0.0), axis=1))
    positions = tok_index - own_start
    cosine, sine_table = rope_tables(positions, HD)
    rot_query = rotate(queries.astype(jnp.float32).reshape(TOKENS, KVH, GROUP, HD), cosine, sine_table).astype(jnp.bfloat16)
    rot_key = rotate(key_value[0].astype(jnp.float32).reshape(TOKENS, KVH, HD), cosine, sine_table).astype(jnp.bfloat16)
    key_cache = rot_key.reshape(TOKENS, KVH * HD)
    value_rows = key_value[1].reshape(TOKENS, KVH, HD)
    pad_keys = jnp.concatenate([jnp.zeros((LMAX, KVH, HD), jnp.bfloat16), rot_key], axis=0)
    pad_values = jnp.concatenate([jnp.zeros((LMAX, KVH, HD), jnp.bfloat16), value_rows], axis=0)
    span = LMAX + TOK_DEV
    scale = HD ** (-0.5)

    def attend_block(block):
        low = block * TOK_DEV
        q_block = lax.dynamic_slice_in_dim(rot_query, low, TOK_DEV, 0)
        k_block = lax.dynamic_slice_in_dim(pad_keys, low, span, 0)
        v_block = lax.dynamic_slice_in_dim(pad_values, low, span, 0)
        q_index = lax.dynamic_slice_in_dim(tok_index, low, TOK_DEV, 0)
        q_start = lax.dynamic_slice_in_dim(own_start, low, TOK_DEV, 0)
        k_index = (low - LMAX).astype(jnp.float32) + jnp.arange(span, dtype=jnp.float32)
        allowed = (k_index[None, :] >= q_start[:, None]) & (k_index[None, :] <= q_index[:, None])
        scores = jnp.einsum('qhgd,khd->hgqk', q_block.astype(jnp.float32), k_block.astype(jnp.float32)) * scale
        scores = jnp.where(allowed[None, None], scores, masked_score)
        peak = lax.optimization_barrier(jnp.max(scores, axis=3, keepdims=True))
        weights = jnp.exp(scores - peak)
        total = lax.optimization_barrier(jnp.sum(weights, axis=3))
        rounded = lax.optimization_barrier(weights.astype(jnp.bfloat16)).astype(jnp.float32)
        context = jnp.einsum('hgqk,khd->qhgd', rounded, v_block.astype(jnp.float32))
        context = context / jnp.transpose(total, (2, 0, 1))[..., None]
        return context.astype(jnp.bfloat16).reshape(TOK_DEV, QH * HD)
    attended = lax.map(attend_block, jnp.arange(TOKENS // TOK_DEV, dtype=jnp.int32)).reshape(TOKENS, QH * HD)
    share = QH * HD // N_TP
    projected = jnp.zeros((TOKENS, D), jnp.float32)
    for rank in range(N_TP):
        part_sum = jnp.dot(attended[:, rank * share:(rank + 1) * share], out_weight[rank * share:(rank + 1) * share], preferred_element_type=jnp.float32)
        projected = projected + lax.optimization_barrier(part_sum.astype(jnp.bfloat16)).astype(jnp.float32)
    hidden = (residual.astype(jnp.float32) + projected).astype(jnp.bfloat16)
    ends = (starts + lengths - 1.0).astype(jnp.int32)
    last_state = hidden[ends].astype(jnp.float32)
    mean_square = lax.optimization_barrier(jnp.sum(last_state * last_state, axis=1)) / D
    last_norm = jnp.sqrt(mean_square)
    scaled = (last_state * head_gain.astype(jnp.float32)).astype(jnp.bfloat16)
    raw = jnp.dot(scaled, vocab_weight, preferred_element_type=jnp.float32)
    top_logit = lax.optimization_barrier(jnp.max(raw * lax.rsqrt(mean_square + eps)[:, None], axis=1))
    return (hidden, key_cache, last_norm, top_logit)
```

```python
import math

import jax
import jax.numpy as jnp
from jax import lax
from jax.experimental import pallas as pl
from jax.experimental.pallas import tpu as pltpu
from jax.sharding import PartitionSpec as P

D = 7168
HD = 128
GROUP = 7
REACH = 4


theta = 5000000.0
eps = 1e-05
masked_score = -1e30


def from_behind(value, axis, steps):
    count = lax.axis_size(axis)
    initial, last = (max(0, -steps), min(count, count - steps))
    return lax.ppermute(value, axis, [(source, source + steps) for source in range(initial, last)])


def rope_tables(positions, width):
    half_width = width // 2
    frequency = theta ** (-(jnp.arange(half_width, dtype=jnp.float32) * 2.0 / width))
    angles = positions[:, None] * frequency[None, :]
    return (jnp.cos(angles), jnp.sin(angles))


def attend_kernel(seg_start, cosine, sine, queries, b4, b3, b2, b1, b0, attended, cache, bias, keys, values):
    rows = queries.shape[0]
    span = keys.shape[0]

    @pl.when(pl.program_id(0) == 0)
    def _():
        key_at = lax.broadcasted_iota(jnp.int32, (rows, span), 1)
        query_at = lax.broadcasted_iota(jnp.int32, (rows, span), 0) + (span - rows)
        keep = (key_at >= seg_start[...]) & (key_at <= query_at)
        bias[...] = jnp.where(keep, 0.0, masked_score)

    for at, block in enumerate((b4, b3, b2, b1, b0)):
        place = pl.ds(at * rows, rows)
        part = block[0].astype(jnp.float32)
        turned = part * cosine[place, :] + pltpu.roll(part, HD // 2, 1) * sine[place, :]
        keys[place, :] = turned.astype(jnp.bfloat16)
        values[place, :] = block[1]
    cache[...] = keys[pl.ds(span - rows, rows), :]
    own_cosine = cosine[pl.ds(span - rows, rows), :]
    own_sine = sine[pl.ds(span - rows, rows), :]
    rate = HD ** (-0.5) * math.log2(math.e)
    for head in range(GROUP):
        lanes = pl.ds(head * HD, HD)
        part = queries[:, lanes].astype(jnp.float32)
        turned = part * own_cosine + pltpu.roll(part, HD // 2, 1) * own_sine
        scores = lax.dot_general(
            turned.astype(jnp.bfloat16),
            keys[...],
            (((1,), (1,)), ((), ())),
            preferred_element_type=jnp.float32,
        )
        scores = scores + bias[...]
        peak = jnp.max(scores, axis=1, keepdims=True)
        weights = jnp.exp2((scores - peak) * rate)
        total = jnp.sum(weights, axis=1, keepdims=True)
        context = jnp.dot(
            weights.astype(jnp.bfloat16), values[...], preferred_element_type=jnp.float32
        )
        attended[:, lanes] = (context / total).astype(jnp.bfloat16)


def attend(seg_start, cosine, sine, queries, blocks):
    rows, width = queries.shape
    heads_kv = width // (GROUP * HD)
    span = cosine.shape[0]
    whole = lambda h: (0, 0)
    block_spec = pl.BlockSpec((2, rows, HD), lambda h: (0, 0, h))
    return pl.pallas_call(
        attend_kernel,
        grid=(heads_kv,),
        in_specs=[
            pl.BlockSpec((rows, 1), whole),
            pl.BlockSpec((span, HD), whole),
            pl.BlockSpec((span, HD), whole),
            pl.BlockSpec((rows, GROUP * HD), lambda h: (0, h)),
        ]
        + [block_spec] * (REACH + 1),
        out_specs=[
            pl.BlockSpec((rows, GROUP * HD), lambda h: (0, h)),
            pl.BlockSpec((rows, HD), lambda h: (0, h)),
        ],
        out_shape=[
            jax.ShapeDtypeStruct((rows, width), jnp.bfloat16),
            jax.ShapeDtypeStruct((rows, heads_kv * HD), jnp.bfloat16),
        ],
        scratch_shapes=[
            pltpu.VMEM((rows, span), jnp.float32),
            pltpu.VMEM((span, HD), jnp.bfloat16),
            pltpu.VMEM((span, HD), jnp.bfloat16),
        ],
        compiler_params=pltpu.CompilerParams(vmem_limit_bytes=40 * 2**20),
        cost_estimate=pl.CostEstimate(
            flops=4 * rows * span * width,
            bytes_accessed=4 * rows * width,
            transcendentals=rows * span * width // HD,
        ),
    )(seg_start, cosine, sine, queries, *blocks)


def project_by_weights(attended, out_weight, residual):
    projected = jnp.dot(
        attended,
        lax.all_gather(out_weight, "req", axis=1, tiled=True),
        preferred_element_type=jnp.float32,
    )
    width_dev = residual.shape[1]
    own_share = lax.psum_scatter(
        projected.astype(jnp.bfloat16), "tp", scatter_dimension=1, tiled=True
    ).astype(jnp.float32)
    return (residual.astype(jnp.float32) + own_share).astype(jnp.bfloat16)


def project_by_plane(attended, out_weight, residual):
    plane = 4
    depth = lax.axis_size("req") // plane
    groups = [[z * plane + i for i in range(plane)] for z in range(depth)]
    weights = lax.all_gather(out_weight, "req", axis_index_groups=groups)
    z = lax.axis_index("req") // plane
    y = lax.axis_index("tp")
    up, down = {}, {}
    forth = back = attended
    for step in range(1, depth):
        forth = from_behind(forth, "req", plane)
        back = from_behind(back, "req", -plane)
        up[step], down[step] = back, forth
    tokens = [
        attended,
        jnp.where(z % 2 == 0, up[1], down[1]),
        jnp.where(z < 2, up[2], down[2]),
        jnp.where(
            z == 0, up[3], jnp.where(z == 1, up[1], jnp.where(z == 2, down[1], down[3]))
        ),
    ]
    half = plane // 2
    kept_weights = lax.dynamic_slice_in_dim(weights, y * half, half, 0)
    sent_weights = lax.dynamic_slice_in_dim(weights, (1 - y) * half, half, 0)

    def product(rows, held):
        parts = [
            jnp.dot(rows, held[i], preferred_element_type=jnp.float32) for i in range(half)
        ]
        return jnp.concatenate(parts, axis=1)

    sums = []
    for rows in tokens:
        sent = product(rows, sent_weights).astype(jnp.bfloat16)
        kept = product(rows, kept_weights)
        came = lax.ppermute(sent, "tp", [(0, 1), (1, 0)])
        sums.append((kept + came.astype(jnp.float32)).astype(jnp.bfloat16))
    pieces = []
    for step in (0, 2, 1, 3):
        piece = jnp.where(y == 0, sums[step], sums[step ^ 2])
        moves = []
        for at in range(depth):
            for i in range(plane):
                for side in range(2):
                    to = at ^ step ^ (2 * side)
                    moves.append(((at * plane + i) * 2 + side, (to * plane + i) * 2 + at // 2))
        pieces.append((step, lax.ppermute(piece, ("req", "tp"), moves)))
    order = []
    for low in range(2):
        for side in range(2):
            step = z ^ (2 * y + low) ^ (2 * side)
            piece = pieces[0][1]
            for number, value in pieces[1:]:
                piece = jnp.where(step == number, value, piece)
            order.append(piece)
    return (residual.astype(jnp.float32) + jnp.concatenate(order, axis=1).astype(jnp.float32)).astype(
        jnp.bfloat16
    )


def local(queries, key_value, segment, residual, out_weight, head_gain, vocab_weight):
    tok_rows = segment.shape[0]
    requests = lax.axis_size("req") // 2
    device = lax.axis_index("req")
    request_ids = jnp.arange(requests, dtype=jnp.int32)
    segments = [from_behind(segment, "req", steps) for steps in range(REACH, 0, -1)] + [segment]
    blocks = [from_behind(key_value, "req", steps) for steps in range(REACH, 0, -1)] + [key_value]
    following = from_behind(segment, "req", -1)
    near = jnp.concatenate(segments)
    span = near.shape[0]
    at = jnp.arange(span, dtype=jnp.int32)
    real = at + (device - REACH) * tok_rows >= 0
    member = near[:, None] == request_ids[None, :]
    first = jnp.min(jnp.where(member & real[:, None], at[:, None], span), axis=0)
    start_at = jnp.sum(jnp.where(member, first[None, :], 0), axis=1)
    cosine, sine_table = rope_tables((at - start_at).astype(jnp.float32), HD)
    cosine = jnp.concatenate([cosine, cosine], axis=1)
    sine_table = jnp.concatenate([-sine_table, sine_table], axis=1)
    attended, key_cache = attend(
        start_at[span - tok_rows :, None], cosine, sine_table, queries, blocks
    )
    if lax.axis_size("req") == 16 and lax.axis_size("tp") == 2:
        hidden = project_by_plane(attended, out_weight, residual)
    else:
        hidden = project_by_weights(attended, out_weight, residual)
    after = jnp.concatenate([segment[1:], following[:1]])
    final = (device == lax.axis_size("req") - 1) & (jnp.arange(tok_rows) == tok_rows - 1)
    is_end = (segment != after) | final
    select = (is_end[:, None] & (segment[:, None] == request_ids[None, :])).astype(jnp.bfloat16)
    local_last = lax.dot_general(
        select, hidden, (((0,), (0,)), ((), ())), preferred_element_type=jnp.float32
    )
    last_state = lax.psum(local_last, "req")
    scaled = (last_state * head_gain.astype(jnp.float32)).astype(jnp.bfloat16)
    square_part = jnp.sum(last_state * last_state, axis=1)
    logit_part = jnp.dot(scaled, vocab_weight, preferred_element_type=jnp.float32)
    square_sum, raw_logits = (
        lax.psum(square_part.astype(jnp.bfloat16), "tp").astype(jnp.float32),
        lax.psum(logit_part.astype(jnp.bfloat16), "tp").astype(jnp.float32),
    )
    mean_square = square_sum / D
    last_norm = jnp.sqrt(mean_square)
    local_top = jnp.max(raw_logits * lax.rsqrt(mean_square + eps)[:, None], axis=1)
    top_logit = lax.pmax(local_top, "req")
    return (hidden, key_cache, last_norm, top_logit)


def solution(mesh):
    placed = (
        P("req", "tp"),
        P(None, "req", "tp"),
        P("req"),
        P("req", "tp"),
        P("tp", "req"),
        P("tp"),
        P("tp", "req"),
    )
    return jax.shard_map(
        local,
        mesh=mesh,
        in_specs=placed,
        out_specs=(P("req", "tp"), P("req", "tp"), P(), P()),
        check_vma=False,
    )
```

```python
import functools
import math

import jax
import jax.numpy as jnp
from jax import lax
from jax.experimental import pallas as pl
from jax.experimental.pallas import tpu as pltpu
from jax.sharding import PartitionSpec as P

D = 7168
HD = 128
GROUP = 7
REACH = 4


theta = 5000000.0
eps = 1e-05
masked_score = -1e30


def from_behind(value, axis, steps):
    count = lax.axis_size(axis)
    initial, last = (max(0, -steps), min(count, count - steps))
    return lax.ppermute(value, axis, [(source, source + steps) for source in range(initial, last)])


def rope_tables(positions, width):
    half_width = width // 2
    frequency = theta ** (-(jnp.arange(half_width, dtype=jnp.float32) * 2.0 / width))
    angles = positions[:, None] * frequency[None, :]
    return (jnp.cos(angles), jnp.sin(angles))


def attend_kernel(seg_start, cosine, sine, queries, b4, b3, b2, b1, b0, attended, cache, bias, keys, values):
    rows = queries.shape[0]
    span = keys.shape[0]

    @pl.when(pl.program_id(0) == 0)
    def _():
        key_at = lax.broadcasted_iota(jnp.int32, (rows, span), 1)
        query_at = lax.broadcasted_iota(jnp.int32, (rows, span), 0) + (span - rows)
        keep = (key_at >= seg_start[...]) & (key_at <= query_at)
        bias[...] = jnp.where(keep, 0.0, masked_score)

    for at, block in enumerate((b4, b3, b2, b1, b0)):
        place = pl.ds(at * rows, rows)
        part = block[0].astype(jnp.float32)
        turned = part * cosine[place, :] + pltpu.roll(part, HD // 2, 1) * sine[place, :]
        keys[place, :] = turned.astype(jnp.bfloat16)
        values[place, :] = block[1]
    cache[...] = keys[pl.ds(span - rows, rows), :]
    own_cosine = cosine[pl.ds(span - rows, rows), :]
    own_sine = sine[pl.ds(span - rows, rows), :]
    rate = HD ** (-0.5) * math.log2(math.e)
    for head in range(GROUP):
        lanes = pl.ds(head * HD, HD)
        part = queries[:, lanes].astype(jnp.float32)
        turned = part * own_cosine + pltpu.roll(part, HD // 2, 1) * own_sine
        scores = lax.dot_general(
            turned.astype(jnp.bfloat16),
            keys[...],
            (((1,), (1,)), ((), ())),
            preferred_element_type=jnp.float32,
        )
        scores = scores + bias[...]
        peak = jnp.max(scores, axis=1, keepdims=True)
        weights = jnp.exp2((scores - peak) * rate)
        total = jnp.sum(weights, axis=1, keepdims=True)
        context = jnp.dot(
            weights.astype(jnp.bfloat16), values[...], preferred_element_type=jnp.float32
        )
        attended[0, :, lanes] = (context / total).astype(jnp.bfloat16)


def attend(seg_start, cosine, sine, queries, blocks):
    rows, width = queries.shape
    heads_kv = width // (GROUP * HD)
    span = cosine.shape[0]
    whole = lambda h: (0, 0)
    block_spec = pl.BlockSpec((2, rows, HD), lambda h: (0, 0, h))
    return pl.pallas_call(
        attend_kernel,
        grid=(heads_kv,),
        in_specs=[
            pl.BlockSpec((rows, 1), whole),
            pl.BlockSpec((span, HD), whole),
            pl.BlockSpec((span, HD), whole),
            pl.BlockSpec((rows, GROUP * HD), lambda h: (0, h)),
        ]
        + [block_spec] * (REACH + 1),
        out_specs=[
            pl.BlockSpec((1, rows, GROUP * HD), lambda h: (h, 0, 0)),
            pl.BlockSpec((rows, HD), lambda h: (0, h)),
        ],
        out_shape=[
            jax.ShapeDtypeStruct((heads_kv, rows, GROUP * HD), jnp.bfloat16),
            jax.ShapeDtypeStruct((rows, heads_kv * HD), jnp.bfloat16),
        ],
        scratch_shapes=[
            pltpu.VMEM((rows, span), jnp.float32),
            pltpu.VMEM((span, HD), jnp.bfloat16),
            pltpu.VMEM((span, HD), jnp.bfloat16),
        ],
        compiler_params=pltpu.CompilerParams(vmem_limit_bytes=40 * 2**20),
        cost_estimate=pl.CostEstimate(
            flops=4 * rows * span * width,
            bytes_accessed=4 * rows * width,
            transcendentals=rows * span * width // HD,
        ),
    )(seg_start, cosine, sine, queries, *blocks)


def project_by_weights(attended, out_weight, residual):
    attended = jnp.swapaxes(attended, 0, 1).reshape(residual.shape[0], -1)
    projected = jnp.dot(
        attended,
        lax.all_gather(out_weight, "req", axis=1, tiled=True),
        preferred_element_type=jnp.float32,
    )
    width_dev = residual.shape[1]
    own_share = lax.psum_scatter(
        projected.astype(jnp.bfloat16), "tp", scatter_dimension=1, tiled=True
    ).astype(jnp.float32)
    return (residual.astype(jnp.float32) + own_share).astype(jnp.bfloat16)


def plane_kernel(
    attended, weights, share, held, blocks, acc, halves, halves_in, sums, pieces,
    load_sems, z_send, z_recv, y_sems, c_send, c_recv,
):
    chunks, rows, depth = attended.shape
    plane = held.shape[0]
    half = plane // 2
    count = blocks.shape[0]
    me = lax.axis_index("req")
    z, lane = me // plane, me % plane
    y = lax.axis_index("tp")
    other = 1 - y
    at_home = y == z // 2

    def at(to_z, to_y):
        return {"req": to_z * plane + lane, "tp": to_y}

    def load(j, c):
        return pltpu.make_async_copy(
            weights.at[j, pl.ds(c * depth, depth), :], held.at[j, c], load_sems.at[j, c]
        )

    def remote(source, landing, send, receive, target):
        return pltpu.make_async_remote_copy(
            src_ref=source,
            dst_ref=landing,
            send_sem=send,
            recv_sem=receive,
            device_id=target,
            device_id_type=pl.DeviceIdType.MESH,
        )

    def along(source, origin, c, way):
        return remote(
            source,
            blocks.at[origin, c],
            z_send.at[way, origin, c],
            z_recv.at[origin, c],
            at(z + 1 - 2 * way, y),
        )

    def across(origin):
        return remote(
            halves.at[origin], halves_in.at[origin], y_sems.at[0, origin], y_sems.at[1, origin],
            at(z, other),
        )

    def home(origin):
        return remote(
            sums.at[origin], pieces.at[z % 2, y], c_send.at[origin], c_recv.at[z % 2, y],
            at(origin, z // 2),
        )

    def multiply(source, origin, c):
        rows_here = source[...]

        @pl.loop(0, plane)
        def _(j):
            acc[origin, j] += jnp.dot(rows_here, held[j, c], preferred_element_type=jnp.float32)

    def send_half(origin):
        for i in range(half):
            halves[origin, i] = acc[origin, other * half + i].astype(jnp.bfloat16)
        across(origin).start()

    def send_home(origin):
        across(origin).wait()
        for i in range(half):
            sums[origin, i] = (
                acc[origin, y * half + i] + halves_in[origin, i].astype(jnp.float32)
            ).astype(jnp.bfloat16)
        stays = at_home & (origin == z)

        @pl.when(stays)
        def _():
            pieces[z % 2, y] = sums[origin]

        @pl.when(jnp.logical_not(stays))
        def _():
            home(origin).start()

    for j in range(plane):
        for c in range(chunks):
            load(j, c).start()

    barrier = pltpu.get_barrier_semaphore()

    def greet(target):
        pl.semaphore_signal(
            barrier, inc=1, device_id=target, device_id_type=pl.DeviceIdType.MESH
        )

    has_up, has_down = z < count - 1, z > 0

    @pl.when(has_up)
    def _():
        greet(at(z + 1, y))

    @pl.when(has_down)
    def _():
        greet(at(z - 1, y))

    greet(at(z, other))
    for low in range(2):
        for side in range(2):

            @pl.when(jnp.logical_not((2 * y + low == z) & (side == y)))
            def _():
                greet(at(2 * y + low, side))

    @pl.loop(0, count)
    def _(origin):
        @pl.loop(0, plane)
        def _(j):
            acc[origin, j] = jnp.zeros(acc.shape[2:], jnp.float32)

    inner = jnp.where(has_up & has_down, 1, 0)
    pl.semaphore_wait(barrier, 6 + inner - jnp.where(at_home, 1, 0))

    @pl.loop(0, chunks)
    def _(c):
        @pl.when(has_up)
        def _():
            along(attended.at[c], z, c, 0).start()

        @pl.when(has_down)
        def _():
            along(attended.at[c], z, c, 1).start()

    @pl.loop(0, chunks)
    def _(c):
        for j in range(plane):
            load(j, c).wait()
        multiply(attended.at[c], z, c)

    send_half(z)
    for step in range(1, count):
        below, above = z - step, z + step
        from_below, from_above = below >= 0, above < count

        @pl.loop(0, chunks)
        def _(c):
            @pl.when(from_below)
            def _():
                along(blocks.at[below, c], below, c, 0).wait_recv()

                @pl.when(has_up)
                def _():
                    along(blocks.at[below, c], below, c, 0).start()

            @pl.when(from_above)
            def _():
                along(blocks.at[above, c], above, c, 1).wait_recv()

                @pl.when(has_down)
                def _():
                    along(blocks.at[above, c], above, c, 1).start()

            @pl.when(from_below)
            def _():
                multiply(blocks.at[below, c], below, c)

            @pl.when(from_above)
            def _():
                multiply(blocks.at[above, c], above, c)

        @pl.when(from_below)
        def _():
            send_half(below)

        @pl.when(from_above)
        def _():
            send_half(above)

        if step == 1:
            send_home(z)
        else:

            @pl.when(below + 1 >= 0)
            def _():
                send_home(below + 1)

            @pl.when(above - 1 < count)
            def _():
                send_home(above - 1)

    @pl.when(z == count - 1)
    def _():
        send_home(0)

    @pl.when(z == 0)
    def _():
        send_home(count - 1)

    for low in range(2):
        for side in range(2):

            @pl.when(jnp.logical_not((2 * y + low == z) & (side == y)))
            def _():
                remote(
                    sums.at[0], pieces.at[low, side], c_send.at[0], c_recv.at[low, side],
                    at(z, other),
                ).wait_recv()

            share[2 * low + side] = pieces[low, side]

    for origin in range(count):

        @pl.when(jnp.logical_not(at_home & (origin == z)))
        def _():
            home(origin).wait_send()

        @pl.loop(0, chunks)
        def _(c):
            @pl.when(has_up & (origin <= z))
            def _():
                along(blocks.at[origin, c], origin, c, 0).wait_send()

            @pl.when(has_down & (origin >= z))
            def _():
                along(blocks.at[origin, c], origin, c, 1).wait_send()


def project_by_plane(attended, out_weight, residual):
    plane = 4
    count = lax.axis_size("req") // plane
    groups = [[z * plane + i for i in range(plane)] for z in range(count)]
    weights = lax.all_gather(out_weight, "req", axis_index_groups=groups)
    chunks, rows, depth = attended.shape
    width = out_weight.shape[1]
    half = plane // 2
    bf16 = jnp.bfloat16
    share = pl.pallas_call(
        plane_kernel,
        in_specs=[pl.BlockSpec(memory_space=pltpu.VMEM), pl.BlockSpec(memory_space=pl.ANY)],
        out_specs=pl.BlockSpec(memory_space=pltpu.VMEM),
        out_shape=jax.ShapeDtypeStruct((4, half, rows, width), bf16),
        scratch_shapes=[
            pltpu.VMEM((plane, chunks, depth, width), bf16),
            pltpu.VMEM((count, chunks, rows, depth), bf16),
            pltpu.VMEM((count, plane, rows, width), jnp.float32),
            pltpu.VMEM((count, half, rows, width), bf16),
            pltpu.VMEM((count, half, rows, width), bf16),
            pltpu.VMEM((count, half, rows, width), bf16),
            pltpu.VMEM((2, 2, half, rows, width), bf16),
            pltpu.SemaphoreType.DMA((plane, chunks)),
            pltpu.SemaphoreType.DMA((2, count, chunks)),
            pltpu.SemaphoreType.DMA((count, chunks)),
            pltpu.SemaphoreType.DMA((2, count)),
            pltpu.SemaphoreType.DMA((count,)),
            pltpu.SemaphoreType.DMA((2, 2)),
        ],
        compiler_params=pltpu.CompilerParams(
            collective_id=1, has_side_effects=True, vmem_limit_bytes=58 * 2**20
        ),
        cost_estimate=pl.CostEstimate(
            flops=2 * count * plane * rows * width * chunks * depth,
            bytes_accessed=2 * plane * width * chunks * depth,
            transcendentals=0,
        ),
    )(attended, weights)
    own_share = share.reshape(2 * plane, rows, width).swapaxes(0, 1).reshape(residual.shape)
    return (residual.astype(jnp.float32) + own_share.astype(jnp.float32)).astype(bf16)


def partner(axis, step):
    place = lax.axis_index(axis)
    jump = 2**step
    return {axis: place + jump * (1 - 2 * ((place // jump) % 2))}


def exchange(source, landing, sems, place, target):
    copy = pltpu.make_async_remote_copy(
        src_ref=source,
        dst_ref=landing,
        send_sem=sems.at[0, place],
        recv_sem=sems.at[1, place],
        device_id=target,
        device_id_type=pl.DeviceIdType.MESH,
    )
    copy.start()
    copy.wait()


def finish_kernel(
    steps_req, steps_tp, select, hidden, gain, vocab, norm, top, weights, scaled,
    states, states_in, parts, parts_in, tops, tops_in, load_sems, sems,
):
    chunks, chunk, words = weights.shape
    targets = [partner("req", step) for step in range(steps_req)]
    beside = [partner("tp", step) for step in range(steps_tp)]

    def load(k):
        return pltpu.make_async_copy(
            vocab.at[pl.ds(k * chunk, chunk), :], weights.at[k], load_sems.at[k]
        )

    for k in range(chunks):
        load(k).start()
    barrier = pltpu.get_barrier_semaphore()
    for target in targets + beside:
        pl.semaphore_signal(
            barrier, inc=1, device_id=target, device_id_type=pl.DeviceIdType.MESH
        )
    states[0] = lax.dot_general(
        select[...], hidden[...], (((0,), (0,)), ((), ())), preferred_element_type=jnp.float32
    )
    pl.semaphore_wait(barrier, len(targets + beside))
    for step, target in enumerate(targets):
        exchange(states.at[step], states_in.at[step], sems, step, target)
        states[step + 1] = states[step] + states_in[step]
    last_state = states[steps_req]
    scaled[...] = (last_state * gain[...].astype(jnp.float32)).astype(jnp.bfloat16)
    edge = parts.shape[2] - 128
    parts[0] = jnp.zeros(parts.shape[1:], jnp.float32)
    parts[0, :, edge:] = jnp.broadcast_to(
        jnp.sum(last_state * last_state, axis=1, keepdims=True), (parts.shape[1], 128)
    )

    @pl.loop(0, chunks)
    def _(k):
        load(k).wait()
        columns = pl.ds(pl.multiple_of(k * chunk, chunk), chunk)
        parts[0, :, :words] += jnp.dot(
            scaled[:, columns], weights[k], preferred_element_type=jnp.float32
        )

    for step, target in enumerate(beside):
        exchange(parts.at[step], parts_in.at[step], sems, steps_req + step, target)
        parts[step + 1] = parts[step] + parts_in[step]
    mean_square = parts[steps_tp, :, edge:] / D
    norm[...] = jnp.sqrt(mean_square)
    peak = jnp.max(parts[steps_tp, :, :words], axis=1, keepdims=True)
    tops[0] = peak * lax.rsqrt(mean_square + eps)
    for step, target in enumerate(targets):
        exchange(tops.at[step], tops_in.at[step], sems, steps_req + steps_tp + step, target)
        tops[step + 1] = jnp.maximum(tops[step], tops_in[step])
    top[...] = tops[steps_req]


def finish(select, hidden, head_gain, vocab_weight):
    requests = select.shape[1]
    depth, words = vocab_weight.shape
    steps_req = lax.axis_size("req").bit_length() - 1
    steps_tp = lax.axis_size("tp").bit_length() - 1
    chunks = 7
    wide = -(-words // 128) * 128 + 128
    in_vmem = pl.BlockSpec(memory_space=pltpu.VMEM)
    small = jax.ShapeDtypeStruct((requests, 128), jnp.float32)
    norm, top = pl.pallas_call(
        functools.partial(finish_kernel, steps_req, steps_tp),
        in_specs=[in_vmem, in_vmem, in_vmem, pl.BlockSpec(memory_space=pl.ANY)],
        out_specs=[in_vmem, in_vmem],
        out_shape=[small, small],
        scratch_shapes=[
            pltpu.VMEM((chunks, depth // chunks, words), jnp.bfloat16),
            pltpu.VMEM((requests, depth), jnp.bfloat16),
            pltpu.VMEM((steps_req + 1, requests, depth), jnp.float32),
            pltpu.VMEM((steps_req, requests, depth), jnp.float32),
            pltpu.VMEM((steps_tp + 1, requests, wide), jnp.float32),
            pltpu.VMEM((steps_tp, requests, wide), jnp.float32),
            pltpu.VMEM((steps_req + 1, requests, 128), jnp.float32),
            pltpu.VMEM((steps_req, requests, 128), jnp.float32),
            pltpu.SemaphoreType.DMA((chunks,)),
            pltpu.SemaphoreType.DMA((2, 2 * steps_req + steps_tp)),
        ],
        compiler_params=pltpu.CompilerParams(
            collective_id=0, has_side_effects=True, vmem_limit_bytes=48 * 2**20
        ),
        cost_estimate=pl.CostEstimate(
            flops=2 * requests * depth * words,
            bytes_accessed=2 * depth * words,
            transcendentals=0,
        ),
    )(select, hidden, head_gain[None, :], vocab_weight)
    return norm[:, 0], top[:, 0]


def local(queries, key_value, segment, residual, out_weight, head_gain, vocab_weight):
    tok_rows = segment.shape[0]
    requests = lax.axis_size("req") // 2
    device = lax.axis_index("req")
    request_ids = jnp.arange(requests, dtype=jnp.int32)
    segments = [from_behind(segment, "req", steps) for steps in range(REACH, 0, -1)] + [segment]
    blocks = [from_behind(key_value, "req", steps) for steps in range(REACH, 0, -1)] + [key_value]
    following = from_behind(segment, "req", -1)
    near = jnp.concatenate(segments)
    span = near.shape[0]
    at = jnp.arange(span, dtype=jnp.int32)
    real = at + (device - REACH) * tok_rows >= 0
    member = near[:, None] == request_ids[None, :]
    first = jnp.min(jnp.where(member & real[:, None], at[:, None], span), axis=0)
    start_at = jnp.sum(jnp.where(member, first[None, :], 0), axis=1)
    cosine, sine_table = rope_tables((at - start_at).astype(jnp.float32), HD)
    cosine = jnp.concatenate([cosine, cosine], axis=1)
    sine_table = jnp.concatenate([-sine_table, sine_table], axis=1)
    attended, key_cache = attend(
        start_at[span - tok_rows :, None], cosine, sine_table, queries, blocks
    )
    if lax.axis_size("req") == 16 and lax.axis_size("tp") == 2:
        hidden = project_by_plane(attended, out_weight, residual)
    else:
        hidden = project_by_weights(attended, out_weight, residual)
    after = jnp.concatenate([segment[1:], following[:1]])
    final = (device == lax.axis_size("req") - 1) & (jnp.arange(tok_rows) == tok_rows - 1)
    is_end = (segment != after) | final
    select = (is_end[:, None] & (segment[:, None] == request_ids[None, :])).astype(jnp.bfloat16)
    last_norm, top_logit = finish(select, hidden, head_gain, vocab_weight)
    return (hidden, key_cache, last_norm, top_logit)


def solution(mesh):
    placed = (
        P("req", "tp"),
        P(None, "req", "tp"),
        P("req"),
        P("req", "tp"),
        P("tp", "req"),
        P("tp"),
        P("tp", "req"),
    )
    return jax.shard_map(
        local,
        mesh=mesh,
        in_specs=placed,
        out_specs=(P("req", "tp"), P("req", "tp"), P(), P()),
        check_vma=False,
    )
```

```python
import functools
import math

import jax
import jax.numpy as jnp
from jax import lax
from jax.experimental import pallas as pl
from jax.experimental.pallas import tpu as pltpu
from jax.sharding import PartitionSpec as P

D = 7168
HD = 128
GROUP = 7
REACH = 4


theta = 5000000.0
eps = 1e-05
masked_score = -1e30


def from_behind(value, axis, steps):
    count = lax.axis_size(axis)
    initial, last = (max(0, -steps), min(count, count - steps))
    return lax.ppermute(value, axis, [(source, source + steps) for source in range(initial, last)])


def rope_tables(positions, width):
    half_width = width // 2
    frequency = theta ** (-(jnp.arange(half_width, dtype=jnp.float32) * 2.0 / width))
    angles = positions[:, None] * frequency[None, :]
    return (jnp.cos(angles), jnp.sin(angles))


def attend_kernel(seg_start, cosine, sine, queries, b4, b3, b2, b1, b0, attended, cache, bias, keys, values):
    rows = queries.shape[0]
    span = keys.shape[0]

    @pl.when(pl.program_id(0) == 0)
    def _():
        key_at = lax.broadcasted_iota(jnp.int32, (rows, span), 1)
        query_at = lax.broadcasted_iota(jnp.int32, (rows, span), 0) + (span - rows)
        keep = (key_at >= seg_start[...]) & (key_at <= query_at)
        bias[...] = jnp.where(keep, 0.0, masked_score)

    for at, block in enumerate((b4, b3, b2, b1, b0)):
        place = pl.ds(at * rows, rows)
        part = block[0].astype(jnp.float32)
        turned = part * cosine[place, :] + pltpu.roll(part, HD // 2, 1) * sine[place, :]
        keys[place, :] = turned.astype(jnp.bfloat16)
        values[place, :] = block[1]
    cache[...] = keys[pl.ds(span - rows, rows), :]
    own_cosine = cosine[pl.ds(span - rows, rows), :]
    own_sine = sine[pl.ds(span - rows, rows), :]
    rate = HD ** (-0.5) * math.log2(math.e)
    for head in range(GROUP):
        lanes = pl.ds(head * HD, HD)
        part = queries[:, lanes].astype(jnp.float32)
        turned = part * own_cosine + pltpu.roll(part, HD // 2, 1) * own_sine
        scores = lax.dot_general(
            turned.astype(jnp.bfloat16),
            keys[...],
            (((1,), (1,)), ((), ())),
            preferred_element_type=jnp.float32,
        )
        scores = scores + bias[...]
        peak = jnp.max(scores, axis=1, keepdims=True)
        weights = jnp.exp2((scores - peak) * rate)
        total = jnp.sum(weights, axis=1, keepdims=True)
        context = jnp.dot(
            weights.astype(jnp.bfloat16), values[...], preferred_element_type=jnp.float32
        )
        attended[0, :, lanes] = (context / total).astype(jnp.bfloat16)


def attend(seg_start, cosine, sine, queries, blocks):
    rows, width = queries.shape
    heads_kv = width // (GROUP * HD)
    span = cosine.shape[0]
    whole = lambda h: (0, 0)
    block_spec = pl.BlockSpec((2, rows, HD), lambda h: (0, 0, h))
    return pl.pallas_call(
        attend_kernel,
        grid=(heads_kv,),
        in_specs=[
            pl.BlockSpec((rows, 1), whole),
            pl.BlockSpec((span, HD), whole),
            pl.BlockSpec((span, HD), whole),
            pl.BlockSpec((rows, GROUP * HD), lambda h: (0, h)),
        ]
        + [block_spec] * (REACH + 1),
        out_specs=[
            pl.BlockSpec((1, rows, GROUP * HD), lambda h: (h, 0, 0)),
            pl.BlockSpec((rows, HD), lambda h: (0, h)),
        ],
        out_shape=[
            jax.ShapeDtypeStruct((heads_kv, rows, GROUP * HD), jnp.bfloat16),
            jax.ShapeDtypeStruct((rows, heads_kv * HD), jnp.bfloat16),
        ],
        scratch_shapes=[
            pltpu.VMEM((rows, span), jnp.float32),
            pltpu.VMEM((span, HD), jnp.bfloat16),
            pltpu.VMEM((span, HD), jnp.bfloat16),
        ],
        compiler_params=pltpu.CompilerParams(vmem_limit_bytes=40 * 2**20),
        cost_estimate=pl.CostEstimate(
            flops=4 * rows * span * width,
            bytes_accessed=4 * rows * width,
            transcendentals=rows * span * width // HD,
        ),
    )(seg_start, cosine, sine, queries, *blocks)


def project_by_weights(attended, out_weight, residual):
    attended = jnp.swapaxes(attended, 0, 1).reshape(residual.shape[0], -1)
    projected = jnp.dot(
        attended,
        lax.all_gather(out_weight, "req", axis=1, tiled=True),
        preferred_element_type=jnp.float32,
    )
    width_dev = residual.shape[1]
    own_share = lax.psum_scatter(
        projected.astype(jnp.bfloat16), "tp", scatter_dimension=1, tiled=True
    ).astype(jnp.float32)
    return (residual.astype(jnp.float32) + own_share).astype(jnp.bfloat16)


def plane_kernel(
    seg_start, cosine, sine, queries, key_value, out_weight, share, cache,
    attended, bias, keys, values, kv_in,
    held, blocks, acc, halves, halves_in, sums, pieces,
    kv_sems, load_sems, w_send, w_recv, z_send, z_recv, y_sems, c_send, c_recv,
):
    chunks, rows, depth = attended.shape
    plane = held.shape[0]
    half = plane // 2
    count = blocks.shape[0]
    me = lax.axis_index("req")
    z, lane = me // plane, me % plane
    y = lax.axis_index("tp")
    mate = lane + 1 - 2 * (lane % 2)
    facing = (lane + half) % plane
    last = lax.axis_size("req") - 1
    other = 1 - y
    at_home = y == z // 2

    def at(to_z, to_y):
        return {"req": to_z * plane + lane, "tp": to_y}

    def load(c):
        return pltpu.make_async_copy(
            out_weight.at[pl.ds(c * depth, depth), :], held.at[lane, c], load_sems.at[c]
        )

    def remote(source, landing, send, receive, target):
        return pltpu.make_async_remote_copy(
            src_ref=source,
            dst_ref=landing,
            send_sem=send,
            recv_sem=receive,
            device_id=target,
            device_id_type=pl.DeviceIdType.MESH,
        )

    def along(source, origin, c, way):
        return remote(
            source,
            blocks.at[origin, c],
            z_send.at[way, origin, c],
            z_recv.at[origin, c],
            at(z + 1 - 2 * way, y),
        )

    def earlier(steps, target):
        return remote(
            key_value, kv_in.at[steps - 1], kv_sems.at[0, steps - 1], kv_sems.at[1, steps - 1],
            {"req": target},
        )

    def spread(kind, c):
        j = facing if kind == 2 else lane
        source = held.at[facing, c] if kind == 2 else out_weight.at[pl.ds(c * depth, depth), :]
        target = facing if kind == 1 else mate
        return remote(
            source, held.at[j, c], w_send.at[kind, c], w_recv.at[j, c], {"req": z * plane + target}
        )

    def take(j, c):
        remote(
            held.at[j, c], held.at[j, c], w_send.at[0, c], w_recv.at[j, c],
            {"req": z * plane + mate},
        ).wait_recv()

    def across(origin):
        return remote(
            halves.at[origin], halves_in.at[origin], y_sems.at[0, origin], y_sems.at[1, origin],
            at(z, other),
        )

    def home(origin):
        return remote(
            sums.at[origin], pieces.at[z % 2, y], c_send.at[origin], c_recv.at[z % 2, y],
            at(origin, z // 2),
        )

    def multiply(source, origin, c):
        rows_here = source[...]

        @pl.loop(0, plane)
        def _(j):
            acc[origin, j] += jnp.dot(rows_here, held[j, c], preferred_element_type=jnp.float32)

    def send_half(origin):
        for i in range(half):
            halves[origin, i] = acc[origin, other * half + i].astype(jnp.bfloat16)
        across(origin).start()

    def send_home(origin):
        across(origin).wait()
        for i in range(half):
            sums[origin, i] = (
                acc[origin, y * half + i] + halves_in[origin, i].astype(jnp.float32)
            ).astype(jnp.bfloat16)
        stays = at_home & (origin == z)

        @pl.when(stays)
        def _():
            pieces[z % 2, y] = sums[origin]

        @pl.when(jnp.logical_not(stays))
        def _():
            home(origin).start()

    for c in range(chunks):
        load(c).start()

    barrier = pltpu.get_barrier_semaphore()

    def greet(target):
        pl.semaphore_signal(
            barrier, inc=1, device_id=target, device_id_type=pl.DeviceIdType.MESH
        )

    has_up, has_down = z < count - 1, z > 0

    @pl.when(has_up)
    def _():
        greet(at(z + 1, y))

    @pl.when(has_down)
    def _():
        greet(at(z - 1, y))

    greet(at(z, other))
    greet({"req": z * plane + mate})
    greet({"req": z * plane + facing})
    for steps in range(1, REACH + 1):

        @pl.when(me >= steps)
        def _():
            greet({"req": me - steps})

    for low in range(2):
        for side in range(2):

            @pl.when(jnp.logical_not((2 * y + low == z) & (side == y)))
            def _():
                greet(at(2 * y + low, side))

    inner = jnp.where(has_up & has_down, 1, 0)
    behind = jnp.minimum(last - me, REACH)
    pl.semaphore_wait(barrier, 8 + inner + behind - jnp.where(at_home, 1, 0))

    for steps in range(1, REACH + 1):

        @pl.when(me + steps <= last)
        def _():
            earlier(steps, me + steps).start()

    for c in range(chunks):
        spread(1, c).start()
        spread(0, c).start()

    span = keys.shape[0]
    key_at = lax.broadcasted_iota(jnp.int32, (rows, span), 1)
    query_at = lax.broadcasted_iota(jnp.int32, (rows, span), 0) + (span - rows)
    keep = (key_at >= seg_start[...]) & (key_at <= query_at)
    bias[...] = jnp.where(keep, 0.0, masked_score)

    @pl.loop(0, count)
    def _(origin):
        @pl.loop(0, plane)
        def _(j):
            acc[origin, j] = jnp.zeros(acc.shape[2:], jnp.float32)

    for steps in range(1, REACH + 1):

        @pl.when(me < steps)
        def _():
            kv_in[steps - 1] = jnp.zeros(kv_in.shape[1:], jnp.bfloat16)

        @pl.when(me >= steps)
        def _():
            earlier(steps, mate).wait_recv()

    rate = HD ** (-0.5) * math.log2(math.e)

    @pl.loop(0, chunks)
    def _(c):
        lanes_kv = pl.ds(pl.multiple_of(c * HD, HD), HD)
        for number in range(REACH + 1):
            place = pl.ds(number * rows, rows)
            block = key_value if number == REACH else kv_in.at[REACH - 1 - number]
            part = block[0, :, lanes_kv].astype(jnp.float32)
            turned = part * cosine[place, :] + pltpu.roll(part, HD // 2, 1) * sine[place, :]
            keys[place, :] = turned.astype(jnp.bfloat16)
            values[place, :] = block[1, :, lanes_kv]
        own = pl.ds(span - rows, rows)
        cache[:, lanes_kv] = keys[own, :]
        for head in range(GROUP):
            lanes = pl.ds(pl.multiple_of(c * depth + head * HD, HD), HD)
            part = queries[:, lanes].astype(jnp.float32)
            turned = part * cosine[own, :] + pltpu.roll(part, HD // 2, 1) * sine[own, :]
            scores = lax.dot_general(
                turned.astype(jnp.bfloat16),
                keys[...],
                (((1,), (1,)), ((), ())),
                preferred_element_type=jnp.float32,
            )
            scores = scores + bias[...]
            peak = jnp.max(scores, axis=1, keepdims=True)
            weights = jnp.exp2((scores - peak) * rate)
            total = jnp.sum(weights, axis=1, keepdims=True)
            context = jnp.dot(
                weights.astype(jnp.bfloat16), values[...], preferred_element_type=jnp.float32
            )
            attended[c, :, pl.ds(head * HD, HD)] = (context / total).astype(jnp.bfloat16)

        @pl.when(has_up)
        def _():
            along(attended.at[c], z, c, 0).start()

        @pl.when(has_down)
        def _():
            along(attended.at[c], z, c, 1).start()

    @pl.loop(0, chunks)
    def _(c):
        take(facing, c)
        spread(2, c).start()

    @pl.loop(0, chunks)
    def _(c):
        load(c).wait()
        take(mate, c)
        take((mate + half) % plane, c)
        multiply(attended.at[c], z, c)

    send_half(z)
    for step in range(1, count):
        below, above = z - step, z + step
        from_below, from_above = below >= 0, above < count

        @pl.loop(0, chunks)
        def _(c):
            @pl.when(from_below)
            def _():
                along(blocks.at[below, c], below, c, 0).wait_recv()

                @pl.when(has_up)
                def _():
                    along(blocks.at[below, c], below, c, 0).start()

            @pl.when(from_above)
            def _():
                along(blocks.at[above, c], above, c, 1).wait_recv()

                @pl.when(has_down)
                def _():
                    along(blocks.at[above, c], above, c, 1).start()

            @pl.when(from_below)
            def _():
                multiply(blocks.at[below, c], below, c)

            @pl.when(from_above)
            def _():
                multiply(blocks.at[above, c], above, c)

        @pl.when(from_below)
        def _():
            send_half(below)

        @pl.when(from_above)
        def _():
            send_half(above)

        if step == 1:
            send_home(z)
        else:

            @pl.when(below + 1 >= 0)
            def _():
                send_home(below + 1)

            @pl.when(above - 1 < count)
            def _():
                send_home(above - 1)

    @pl.when(z == count - 1)
    def _():
        send_home(0)

    @pl.when(z == 0)
    def _():
        send_home(count - 1)

    for low in range(2):
        for side in range(2):

            @pl.when(jnp.logical_not((2 * y + low == z) & (side == y)))
            def _():
                remote(
                    sums.at[0], pieces.at[low, side], c_send.at[0], c_recv.at[low, side],
                    at(z, other),
                ).wait_recv()

            share[2 * low + side] = pieces[low, side]

    for steps in range(1, REACH + 1):

        @pl.when(me + steps <= last)
        def _():
            earlier(steps, me + steps).wait_send()

    @pl.loop(0, chunks)
    def _(c):
        for kind in range(3):
            spread(kind, c).wait_send()

    for origin in range(count):

        @pl.when(jnp.logical_not(at_home & (origin == z)))
        def _():
            home(origin).wait_send()

        @pl.loop(0, chunks)
        def _(c):
            @pl.when(has_up & (origin <= z))
            def _():
                along(blocks.at[origin, c], origin, c, 0).wait_send()

            @pl.when(has_down & (origin >= z))
            def _():
                along(blocks.at[origin, c], origin, c, 1).wait_send()


def attend_and_project(seg_start, cosine, sine, queries, key_value, out_weight, residual):
    plane = 4
    count = lax.axis_size("req") // plane
    rows = queries.shape[0]
    chunks = key_value.shape[2] // HD
    depth = GROUP * HD
    span = cosine.shape[0]
    width = out_weight.shape[1]
    half = plane // 2
    bf16 = jnp.bfloat16
    in_vmem = pl.BlockSpec(memory_space=pltpu.VMEM)
    share, key_cache = pl.pallas_call(
        plane_kernel,
        in_specs=[in_vmem] * 5 + [pl.BlockSpec(memory_space=pl.ANY)],
        out_specs=[in_vmem, in_vmem],
        out_shape=[
            jax.ShapeDtypeStruct((4, half, rows, width), bf16),
            jax.ShapeDtypeStruct((rows, chunks * HD), bf16),
        ],
        scratch_shapes=[
            pltpu.VMEM((chunks, rows, depth), bf16),
            pltpu.VMEM((rows, span), jnp.float32),
            pltpu.VMEM((span, HD), bf16),
            pltpu.VMEM((span, HD), bf16),
            pltpu.VMEM((REACH,) + key_value.shape, bf16),
            pltpu.VMEM((plane, chunks, depth, width), bf16),
            pltpu.VMEM((count, chunks, rows, depth), bf16),
            pltpu.VMEM((count, plane, rows, width), jnp.float32),
            pltpu.VMEM((count, half, rows, width), bf16),
            pltpu.VMEM((count, half, rows, width), bf16),
            pltpu.VMEM((count, half, rows, width), bf16),
            pltpu.VMEM((2, 2, half, rows, width), bf16),
            pltpu.SemaphoreType.DMA((2, REACH)),
            pltpu.SemaphoreType.DMA((chunks,)),
            pltpu.SemaphoreType.DMA((3, chunks)),
            pltpu.SemaphoreType.DMA((plane, chunks)),
            pltpu.SemaphoreType.DMA((2, count, chunks)),
            pltpu.SemaphoreType.DMA((count, chunks)),
            pltpu.SemaphoreType.DMA((2, count)),
            pltpu.SemaphoreType.DMA((count,)),
            pltpu.SemaphoreType.DMA((2, 2)),
        ],
        compiler_params=pltpu.CompilerParams(
            collective_id=1, has_side_effects=True, vmem_limit_bytes=62 * 2**20
        ),
        cost_estimate=pl.CostEstimate(
            flops=2 * count * plane * rows * width * chunks * depth
            + 4 * rows * span * chunks * depth,
            bytes_accessed=2 * width * chunks * depth,
            transcendentals=rows * span * chunks * GROUP,
        ),
    )(seg_start, cosine, sine, queries, key_value, out_weight)
    own_share = share.reshape(2 * plane, rows, width).swapaxes(0, 1).reshape(residual.shape)
    hidden = (residual.astype(jnp.float32) + own_share.astype(jnp.float32)).astype(bf16)
    return hidden, key_cache


def partner(axis, step):
    place = lax.axis_index(axis)
    jump = 2**step
    return {axis: place + jump * (1 - 2 * ((place // jump) % 2))}


def exchange(source, landing, sems, place, target):
    copy = pltpu.make_async_remote_copy(
        src_ref=source,
        dst_ref=landing,
        send_sem=sems.at[0, place],
        recv_sem=sems.at[1, place],
        device_id=target,
        device_id_type=pl.DeviceIdType.MESH,
    )
    copy.start()
    copy.wait()


def finish_kernel(
    steps_req, steps_tp, select, hidden, gain, vocab, norm, top, weights, scaled,
    states, states_in, parts, parts_in, tops, tops_in, load_sems, sems,
):
    chunks, chunk, words = weights.shape
    targets = [partner("req", step) for step in range(steps_req)]
    beside = [partner("tp", step) for step in range(steps_tp)]

    def load(k):
        return pltpu.make_async_copy(
            vocab.at[pl.ds(k * chunk, chunk), :], weights.at[k], load_sems.at[k]
        )

    for k in range(chunks):
        load(k).start()
    barrier = pltpu.get_barrier_semaphore()
    for target in targets + beside:
        pl.semaphore_signal(
            barrier, inc=1, device_id=target, device_id_type=pl.DeviceIdType.MESH
        )
    states[0] = lax.dot_general(
        select[...], hidden[...], (((0,), (0,)), ((), ())), preferred_element_type=jnp.float32
    )
    pl.semaphore_wait(barrier, len(targets + beside))
    for step, target in enumerate(targets):
        exchange(states.at[step], states_in.at[step], sems, step, target)
        states[step + 1] = states[step] + states_in[step]
    last_state = states[steps_req]
    scaled[...] = (last_state * gain[...].astype(jnp.float32)).astype(jnp.bfloat16)
    edge = parts.shape[2] - 128
    parts[0] = jnp.zeros(parts.shape[1:], jnp.float32)
    parts[0, :, edge:] = jnp.broadcast_to(
        jnp.sum(last_state * last_state, axis=1, keepdims=True), (parts.shape[1], 128)
    )

    @pl.loop(0, chunks)
    def _(k):
        load(k).wait()
        columns = pl.ds(pl.multiple_of(k * chunk, chunk), chunk)
        parts[0, :, :words] += jnp.dot(
            scaled[:, columns], weights[k], preferred_element_type=jnp.float32
        )

    for step, target in enumerate(beside):
        exchange(parts.at[step], parts_in.at[step], sems, steps_req + step, target)
        parts[step + 1] = parts[step] + parts_in[step]
    mean_square = parts[steps_tp, :, edge:] / D
    norm[...] = jnp.sqrt(mean_square)
    peak = jnp.max(parts[steps_tp, :, :words], axis=1, keepdims=True)
    tops[0] = peak * lax.rsqrt(mean_square + eps)
    for step, target in enumerate(targets):
        exchange(tops.at[step], tops_in.at[step], sems, steps_req + steps_tp + step, target)
        tops[step + 1] = jnp.maximum(tops[step], tops_in[step])
    top[...] = tops[steps_req]


def finish(select, hidden, head_gain, vocab_weight):
    requests = select.shape[1]
    depth, words = vocab_weight.shape
    steps_req = lax.axis_size("req").bit_length() - 1
    steps_tp = lax.axis_size("tp").bit_length() - 1
    chunks = 7
    wide = -(-words // 128) * 128 + 128
    in_vmem = pl.BlockSpec(memory_space=pltpu.VMEM)
    small = jax.ShapeDtypeStruct((requests, 128), jnp.float32)
    norm, top = pl.pallas_call(
        functools.partial(finish_kernel, steps_req, steps_tp),
        in_specs=[in_vmem, in_vmem, in_vmem, pl.BlockSpec(memory_space=pl.ANY)],
        out_specs=[in_vmem, in_vmem],
        out_shape=[small, small],
        scratch_shapes=[
            pltpu.VMEM((chunks, depth // chunks, words), jnp.bfloat16),
            pltpu.VMEM((requests, depth), jnp.bfloat16),
            pltpu.VMEM((steps_req + 1, requests, depth), jnp.float32),
            pltpu.VMEM((steps_req, requests, depth), jnp.float32),
            pltpu.VMEM((steps_tp + 1, requests, wide), jnp.float32),
            pltpu.VMEM((steps_tp, requests, wide), jnp.float32),
            pltpu.VMEM((steps_req + 1, requests, 128), jnp.float32),
            pltpu.VMEM((steps_req, requests, 128), jnp.float32),
            pltpu.SemaphoreType.DMA((chunks,)),
            pltpu.SemaphoreType.DMA((2, 2 * steps_req + steps_tp)),
        ],
        compiler_params=pltpu.CompilerParams(
            collective_id=0, has_side_effects=True, vmem_limit_bytes=48 * 2**20
        ),
        cost_estimate=pl.CostEstimate(
            flops=2 * requests * depth * words,
            bytes_accessed=2 * depth * words,
            transcendentals=0,
        ),
    )(select, hidden, head_gain[None, :], vocab_weight)
    return norm[:, 0], top[:, 0]


def local(queries, key_value, segment, residual, out_weight, head_gain, vocab_weight):
    tok_rows = segment.shape[0]
    requests = lax.axis_size("req") // 2
    device = lax.axis_index("req")
    request_ids = jnp.arange(requests, dtype=jnp.int32)
    segments = [from_behind(segment, "req", steps) for steps in range(REACH, 0, -1)] + [segment]
    following = from_behind(segment, "req", -1)
    near = jnp.concatenate(segments)
    span = near.shape[0]
    at = jnp.arange(span, dtype=jnp.int32)
    real = at + (device - REACH) * tok_rows >= 0
    member = near[:, None] == request_ids[None, :]
    first = jnp.min(jnp.where(member & real[:, None], at[:, None], span), axis=0)
    start_at = jnp.sum(jnp.where(member, first[None, :], 0), axis=1)
    cosine, sine_table = rope_tables((at - start_at).astype(jnp.float32), HD)
    cosine = jnp.concatenate([cosine, cosine], axis=1)
    sine_table = jnp.concatenate([-sine_table, sine_table], axis=1)
    own_start = start_at[span - tok_rows :, None]
    if lax.axis_size("req") == 16 and lax.axis_size("tp") == 2:
        hidden, key_cache = attend_and_project(
            own_start, cosine, sine_table, queries, key_value, out_weight, residual
        )
    else:
        blocks = [from_behind(key_value, "req", steps) for steps in range(REACH, 0, -1)]
        attended, key_cache = attend(own_start, cosine, sine_table, queries, blocks + [key_value])
        hidden = project_by_weights(attended, out_weight, residual)
    after = jnp.concatenate([segment[1:], following[:1]])
    final = (device == lax.axis_size("req") - 1) & (jnp.arange(tok_rows) == tok_rows - 1)
    is_end = (segment != after) | final
    select = (is_end[:, None] & (segment[:, None] == request_ids[None, :])).astype(jnp.bfloat16)
    last_norm, top_logit = finish(select, hidden, head_gain, vocab_weight)
    return (hidden, key_cache, last_norm, top_logit)


def solution(mesh):
    placed = (
        P("req", "tp"),
        P(None, "req", "tp"),
        P("req"),
        P("req", "tp"),
        P("tp", "req"),
        P("tp"),
        P("tp", "req"),
    )
    return jax.shard_map(
        local,
        mesh=mesh,
        in_specs=placed,
        out_specs=(P("req", "tp"), P("req", "tp"), P(), P()),
        check_vma=False,
    )
```

```python
import functools
import math

import jax
import jax.numpy as jnp
from jax import lax
from jax.experimental import pallas as pl
from jax.experimental.pallas import tpu as pltpu
from jax.sharding import PartitionSpec as P

D = 7168
HD = 128
GROUP = 7
REACH = 4


theta = 5000000.0
eps = 1e-05
masked_score = -1e30


def from_behind(value, axis, steps):
    count = lax.axis_size(axis)
    initial, last = (max(0, -steps), min(count, count - steps))
    return lax.ppermute(value, axis, [(source, source + steps) for source in range(initial, last)])


def rope_tables(positions, width):
    half_width = width // 2
    frequency = theta ** (-(jnp.arange(half_width, dtype=jnp.float32) * 2.0 / width))
    angles = positions[:, None] * frequency[None, :]
    return (jnp.cos(angles), jnp.sin(angles))


def attend_kernel(seg_start, cosine, sine, queries, b4, b3, b2, b1, b0, attended, cache, bias, keys, values):
    rows = queries.shape[0]
    span = keys.shape[0]

    @pl.when(pl.program_id(0) == 0)
    def _():
        key_at = lax.broadcasted_iota(jnp.int32, (rows, span), 1)
        query_at = lax.broadcasted_iota(jnp.int32, (rows, span), 0) + (span - rows)
        keep = (key_at >= seg_start[...]) & (key_at <= query_at)
        bias[...] = jnp.where(keep, 0.0, masked_score)

    for at, block in enumerate((b4, b3, b2, b1, b0)):
        place = pl.ds(at * rows, rows)
        part = block[0].astype(jnp.float32)
        turned = part * cosine[place, :] + pltpu.roll(part, HD // 2, 1) * sine[place, :]
        keys[place, :] = turned.astype(jnp.bfloat16)
        values[place, :] = block[1]
    cache[...] = keys[pl.ds(span - rows, rows), :]
    own_cosine = cosine[pl.ds(span - rows, rows), :]
    own_sine = sine[pl.ds(span - rows, rows), :]
    rate = HD ** (-0.5) * math.log2(math.e)
    for head in range(GROUP):
        lanes = pl.ds(head * HD, HD)
        part = queries[:, lanes].astype(jnp.float32)
        turned = part * own_cosine + pltpu.roll(part, HD // 2, 1) * own_sine
        scores = lax.dot_general(
            turned.astype(jnp.bfloat16),
            keys[...],
            (((1,), (1,)), ((), ())),
            preferred_element_type=jnp.float32,
        )
        scores = scores + bias[...]
        peak = jnp.max(scores, axis=1, keepdims=True)
        weights = jnp.exp2((scores - peak) * rate)
        total = jnp.sum(weights, axis=1, keepdims=True)
        context = jnp.dot(
            weights.astype(jnp.bfloat16), values[...], preferred_element_type=jnp.float32
        )
        attended[0, :, lanes] = (context / total).astype(jnp.bfloat16)


def attend(seg_start, cosine, sine, queries, blocks):
    rows, width = queries.shape
    heads_kv = width // (GROUP * HD)
    span = cosine.shape[0]
    whole = lambda h: (0, 0)
    block_spec = pl.BlockSpec((2, rows, HD), lambda h: (0, 0, h))
    return pl.pallas_call(
        attend_kernel,
        grid=(heads_kv,),
        in_specs=[
            pl.BlockSpec((rows, 1), whole),
            pl.BlockSpec((span, HD), whole),
            pl.BlockSpec((span, HD), whole),
            pl.BlockSpec((rows, GROUP * HD), lambda h: (0, h)),
        ]
        + [block_spec] * (REACH + 1),
        out_specs=[
            pl.BlockSpec((1, rows, GROUP * HD), lambda h: (h, 0, 0)),
            pl.BlockSpec((rows, HD), lambda h: (0, h)),
        ],
        out_shape=[
            jax.ShapeDtypeStruct((heads_kv, rows, GROUP * HD), jnp.bfloat16),
            jax.ShapeDtypeStruct((rows, heads_kv * HD), jnp.bfloat16),
        ],
        scratch_shapes=[
            pltpu.VMEM((rows, span), jnp.float32),
            pltpu.VMEM((span, HD), jnp.bfloat16),
            pltpu.VMEM((span, HD), jnp.bfloat16),
        ],
        compiler_params=pltpu.CompilerParams(vmem_limit_bytes=40 * 2**20),
        cost_estimate=pl.CostEstimate(
            flops=4 * rows * span * width,
            bytes_accessed=4 * rows * width,
            transcendentals=rows * span * width // HD,
        ),
    )(seg_start, cosine, sine, queries, *blocks)


def project_by_weights(attended, out_weight, residual):
    attended = jnp.swapaxes(attended, 0, 1).reshape(residual.shape[0], -1)
    projected = jnp.dot(
        attended,
        lax.all_gather(out_weight, "req", axis=1, tiled=True),
        preferred_element_type=jnp.float32,
    )
    width_dev = residual.shape[1]
    own_share = lax.psum_scatter(
        projected.astype(jnp.bfloat16), "tp", scatter_dimension=1, tiled=True
    ).astype(jnp.float32)
    return (residual.astype(jnp.float32) + own_share).astype(jnp.bfloat16)


def plane_kernel(
    seg_start, cosine, sine, queries, key_value, residual, out_weight, hidden, cache,
    attended, bias, keys, values, kv_in,
    held, blocks, acc, halves, halves_in, sums, pieces,
    kv_sems, load_sems, w_send, w_recv, z_send, z_recv, y_sems, c_send, c_recv,
):
    chunks, rows, depth = attended.shape
    plane = 4
    half = plane // 2
    width = out_weight.shape[0]
    wide = half * width
    count = blocks.shape[0]
    me = lax.axis_index("req")
    z, lane = me // plane, me % plane
    y = lax.axis_index("tp")
    mate = lane + 1 - 2 * (lane % 2)
    facing = (lane + half) % plane
    last = lax.axis_size("req") - 1
    other = 1 - y
    at_home = y == z // 2

    def at(to_z, to_y):
        return {"req": to_z * plane + lane, "tp": to_y}

    def strip(c):
        return out_weight.at[:, pl.ds(pl.multiple_of(c * depth, 128), depth)]

    def slot(j, c):
        return held.at[c, pl.ds(pl.multiple_of(j * width, 16), width), :]

    def load(c):
        return pltpu.make_async_copy(strip(c), slot(lane, c), load_sems.at[c])

    def remote(source, landing, send, receive, target):
        return pltpu.make_async_remote_copy(
            src_ref=source,
            dst_ref=landing,
            send_sem=send,
            recv_sem=receive,
            device_id=target,
            device_id_type=pl.DeviceIdType.MESH,
        )

    def along(source, origin, c, way):
        return remote(
            source,
            blocks.at[origin, c],
            z_send.at[way, origin, c],
            z_recv.at[origin, c],
            at(z + 1 - 2 * way, y),
        )

    def earlier(steps, target):
        return remote(
            key_value, kv_in.at[steps - 1], kv_sems.at[0, steps - 1], kv_sems.at[1, steps - 1],
            {"req": target},
        )

    def spread(kind, c):
        j = facing if kind == 2 else lane
        source = slot(facing, c) if kind == 2 else strip(c)
        target = facing if kind == 1 else mate
        return remote(
            source, slot(j, c), w_send.at[kind, c], w_recv.at[j, c], {"req": z * plane + target}
        )

    def take(j, c):
        remote(
            slot(j, c), slot(j, c), w_send.at[0, c], w_recv.at[j, c],
            {"req": z * plane + mate},
        ).wait_recv()

    def across(origin):
        return remote(
            halves.at[origin], halves_in.at[origin], y_sems.at[0, origin], y_sems.at[1, origin],
            at(z, other),
        )

    def home(origin):
        return remote(
            sums.at[origin], pieces.at[z % 2, y], c_send.at[origin], c_recv.at[z % 2, y],
            at(origin, z // 2),
        )

    def multiply(source, origin, c):
        rows_here = source[...]

        @pl.loop(0, 2)
        def _(i):
            acc[origin, i] += lax.dot_general(
                rows_here,
                held[c, pl.ds(pl.multiple_of(i * wide, 16), wide), :],
                (((1,), (1,)), ((), ())),
                preferred_element_type=jnp.float32,
            )

    def send_half(origin):
        halves[origin] = acc[origin, other].astype(jnp.bfloat16)
        across(origin).start()

    def send_home(origin):
        across(origin).wait()
        sums[origin] = (acc[origin, y] + halves_in[origin].astype(jnp.float32)).astype(
            jnp.bfloat16
        )
        stays = at_home & (origin == z)

        @pl.when(stays)
        def _():
            pieces[z % 2, y] = sums[origin]

        @pl.when(jnp.logical_not(stays))
        def _():
            home(origin).start()

    for c in range(chunks):
        load(c).start()

    barrier = pltpu.get_barrier_semaphore()

    def greet(target):
        pl.semaphore_signal(
            barrier, inc=1, device_id=target, device_id_type=pl.DeviceIdType.MESH
        )

    has_up, has_down = z < count - 1, z > 0

    @pl.when(has_up)
    def _():
        greet(at(z + 1, y))

    @pl.when(has_down)
    def _():
        greet(at(z - 1, y))

    greet(at(z, other))
    greet({"req": z * plane + mate})
    greet({"req": z * plane + facing})
    for steps in range(1, REACH + 1):

        @pl.when(me >= steps)
        def _():
            greet({"req": me - steps})

    for low in range(2):
        for side in range(2):

            @pl.when(jnp.logical_not((2 * y + low == z) & (side == y)))
            def _():
                greet(at(2 * y + low, side))

    inner = jnp.where(has_up & has_down, 1, 0)
    behind = jnp.minimum(last - me, REACH)
    pl.semaphore_wait(barrier, 8 + inner + behind - jnp.where(at_home, 1, 0))

    for steps in range(1, REACH + 1):

        @pl.when(me + steps <= last)
        def _():
            earlier(steps, me + steps).start()

    for c in range(chunks):
        spread(1, c).start()
        spread(0, c).start()

    span = keys.shape[0]
    key_at = lax.broadcasted_iota(jnp.int32, (rows, span), 1)
    query_at = lax.broadcasted_iota(jnp.int32, (rows, span), 0) + (span - rows)
    keep = (key_at >= seg_start[...]) & (key_at <= query_at)
    bias[...] = jnp.where(keep, 0.0, masked_score)

    @pl.loop(0, count)
    def _(origin):
        for i in range(2):
            acc[origin, i] = jnp.zeros(acc.shape[2:], jnp.float32)

    for steps in range(1, REACH + 1):

        @pl.when(me < steps)
        def _():
            kv_in[steps - 1] = jnp.zeros(kv_in.shape[1:], jnp.bfloat16)

        @pl.when(me >= steps)
        def _():
            earlier(steps, mate).wait_recv()

    rate = HD ** (-0.5) * math.log2(math.e)

    @pl.loop(0, chunks)
    def _(c):
        lanes_kv = pl.ds(pl.multiple_of(c * HD, HD), HD)
        for number in range(REACH + 1):
            place = pl.ds(number * rows, rows)
            block = key_value if number == REACH else kv_in.at[REACH - 1 - number]
            part = block[0, :, lanes_kv].astype(jnp.float32)
            turned = part * cosine[place, :] + pltpu.roll(part, HD // 2, 1) * sine[place, :]
            keys[place, :] = turned.astype(jnp.bfloat16)
            values[place, :] = block[1, :, lanes_kv]
        own = pl.ds(span - rows, rows)
        cache[:, lanes_kv] = keys[own, :]
        for head in range(GROUP):
            lanes = pl.ds(pl.multiple_of(c * depth + head * HD, HD), HD)
            part = queries[:, lanes].astype(jnp.float32)
            turned = part * cosine[own, :] + pltpu.roll(part, HD // 2, 1) * sine[own, :]
            scores = lax.dot_general(
                turned.astype(jnp.bfloat16),
                keys[...],
                (((1,), (1,)), ((), ())),
                preferred_element_type=jnp.float32,
            )
            scores = scores + bias[...]
            peak = jnp.max(scores, axis=1, keepdims=True)
            weights = jnp.exp2((scores - peak) * rate)
            total = jnp.sum(weights, axis=1, keepdims=True)
            context = jnp.dot(
                weights.astype(jnp.bfloat16), values[...], preferred_element_type=jnp.float32
            )
            attended[c, :, pl.ds(head * HD, HD)] = (context / total).astype(jnp.bfloat16)

        @pl.when(has_up)
        def _():
            along(attended.at[c], z, c, 0).start()

        @pl.when(has_down)
        def _():
            along(attended.at[c], z, c, 1).start()

    @pl.loop(0, chunks)
    def _(c):
        take(facing, c)
        spread(2, c).start()

    def of_blocks(step, act):
        @pl.when(z - step >= 0)
        def _():
            act(z - step)

        @pl.when(z + step < count)
        def _():
            act(z + step)

    for step in range(1, count):
        below, above = z - step, z + step
        from_below, from_above = below >= 0, above < count

        @pl.loop(0, chunks)
        def _(c):
            @pl.when(from_below)
            def _():
                along(blocks.at[below, c], below, c, 0).wait_recv()

                @pl.when(has_up)
                def _():
                    along(blocks.at[below, c], below, c, 0).start()

            @pl.when(from_above)
            def _():
                along(blocks.at[above, c], above, c, 1).wait_recv()

                @pl.when(has_down)
                def _():
                    along(blocks.at[above, c], above, c, 1).start()

            if step == 1:
                load(c).wait()
                take(mate, c)
                take((mate + half) % plane, c)
                multiply(attended.at[c], z, c)
            if step > 1:
                of_blocks(step - 1, lambda origin: multiply(blocks.at[origin, c], origin, c))
            if step == count - 1:
                of_blocks(step, lambda origin: multiply(blocks.at[origin, c], origin, c))

        if step == 1:
            send_half(z)
        if step == 2:
            of_blocks(1, send_half)
            send_home(z)
        if step == 3:
            of_blocks(2, send_half)
            of_blocks(3, send_half)
            of_blocks(1, send_home)
            of_blocks(2, send_home)
            of_blocks(3, send_home)

    for low in range(2):
        for side in range(2):

            @pl.when(jnp.logical_not((2 * y + low == z) & (side == y)))
            def _():
                remote(
                    sums.at[0], pieces.at[low, side], c_send.at[0], c_recv.at[low, side],
                    at(z, other),
                ).wait_recv()

            columns = pl.ds((2 * low + side) * wide, wide)
            hidden[:, columns] = (
                residual[:, columns].astype(jnp.float32) + pieces[low, side].astype(jnp.float32)
            ).astype(jnp.bfloat16)

    for steps in range(1, REACH + 1):

        @pl.when(me + steps <= last)
        def _():
            earlier(steps, me + steps).wait_send()

    @pl.loop(0, chunks)
    def _(c):
        for kind in range(3):
            spread(kind, c).wait_send()

    for origin in range(count):

        @pl.when(jnp.logical_not(at_home & (origin == z)))
        def _():
            home(origin).wait_send()

        @pl.loop(0, chunks)
        def _(c):
            @pl.when(has_up & (origin <= z))
            def _():
                along(blocks.at[origin, c], origin, c, 0).wait_send()

            @pl.when(has_down & (origin >= z))
            def _():
                along(blocks.at[origin, c], origin, c, 1).wait_send()


def attend_and_project(seg_start, cosine, sine, queries, key_value, out_weight, residual):
    plane = 4
    count = lax.axis_size("req") // plane
    rows = queries.shape[0]
    chunks = key_value.shape[2] // HD
    depth = GROUP * HD
    span = cosine.shape[0]
    width = out_weight.shape[1]
    half = plane // 2
    bf16 = jnp.bfloat16
    in_vmem = pl.BlockSpec(memory_space=pltpu.VMEM)
    hidden, key_cache = pl.pallas_call(
        plane_kernel,
        in_specs=[in_vmem] * 6 + [pl.BlockSpec(memory_space=pl.ANY)],
        out_specs=[in_vmem, in_vmem],
        out_shape=[
            jax.ShapeDtypeStruct(residual.shape, bf16),
            jax.ShapeDtypeStruct((rows, chunks * HD), bf16),
        ],
        scratch_shapes=[
            pltpu.VMEM((chunks, rows, depth), bf16),
            pltpu.VMEM((rows, span), jnp.float32),
            pltpu.VMEM((span, HD), bf16),
            pltpu.VMEM((span, HD), bf16),
            pltpu.VMEM((REACH,) + key_value.shape, bf16),
            pltpu.VMEM((chunks, plane * width, depth), bf16),
            pltpu.VMEM((count, chunks, rows, depth), bf16),
            pltpu.VMEM((count, 2, rows, half * width), jnp.float32),
            pltpu.VMEM((count, rows, half * width), bf16),
            pltpu.VMEM((count, rows, half * width), bf16),
            pltpu.VMEM((count, rows, half * width), bf16),
            pltpu.VMEM((2, 2, rows, half * width), bf16),
            pltpu.SemaphoreType.DMA((2, REACH)),
            pltpu.SemaphoreType.DMA((chunks,)),
            pltpu.SemaphoreType.DMA((3, chunks)),
            pltpu.SemaphoreType.DMA((plane, chunks)),
            pltpu.SemaphoreType.DMA((2, count, chunks)),
            pltpu.SemaphoreType.DMA((count, chunks)),
            pltpu.SemaphoreType.DMA((2, count)),
            pltpu.SemaphoreType.DMA((count,)),
            pltpu.SemaphoreType.DMA((2, 2)),
        ],
        compiler_params=pltpu.CompilerParams(
            collective_id=1, has_side_effects=True, vmem_limit_bytes=62 * 2**20
        ),
        cost_estimate=pl.CostEstimate(
            flops=2 * count * plane * rows * width * chunks * depth
            + 4 * rows * span * chunks * depth,
            bytes_accessed=2 * width * chunks * depth,
            transcendentals=rows * span * chunks * GROUP,
        ),
    )(seg_start, cosine, sine, queries, key_value, residual, out_weight.T)
    return hidden, key_cache


def partner(axis, step):
    place = lax.axis_index(axis)
    jump = 2**step
    return {axis: place + jump * (1 - 2 * ((place // jump) % 2))}


def exchange(source, landing, sems, place, target):
    copy = pltpu.make_async_remote_copy(
        src_ref=source,
        dst_ref=landing,
        send_sem=sems.at[0, place],
        recv_sem=sems.at[1, place],
        device_id=target,
        device_id_type=pl.DeviceIdType.MESH,
    )
    copy.start()
    copy.wait()


def finish_kernel(
    steps_req, steps_tp, select, hidden, gain, vocab, norm, top, weights, scaled,
    states, states_in, parts, parts_in, tops, tops_in, load_sems, sems,
):
    chunks, chunk, depth = weights.shape
    targets = [partner("req", step) for step in range(steps_req)]
    beside = [partner("tp", step) for step in range(steps_tp)]

    def load(k):
        return pltpu.make_async_copy(
            vocab.at[pl.ds(k * chunk, chunk), :], weights.at[k], load_sems.at[k]
        )

    for k in range(chunks):
        load(k).start()
    barrier = pltpu.get_barrier_semaphore()
    for target in targets + beside:
        pl.semaphore_signal(
            barrier, inc=1, device_id=target, device_id_type=pl.DeviceIdType.MESH
        )
    states[0] = lax.dot_general(
        select[...], hidden[...], (((0,), (0,)), ((), ())), preferred_element_type=jnp.float32
    )
    pl.semaphore_wait(barrier, len(targets + beside))
    for step, target in enumerate(targets):
        exchange(states.at[step], states_in.at[step], sems, step, target)
        states[step + 1] = states[step] + states_in[step]
    last_state = states[steps_req]
    scaled[...] = (last_state * gain[...].astype(jnp.float32)).astype(jnp.bfloat16)
    parts[0, chunks] = jnp.broadcast_to(
        jnp.sum(last_state * last_state, axis=1, keepdims=True), parts.shape[2:]
    )

    @pl.loop(0, chunks)
    def _(k):
        load(k).wait()
        parts[0, k] = lax.dot_general(
            scaled[...],
            weights[k],
            (((1,), (1,)), ((), ())),
            preferred_element_type=jnp.float32,
        )

    for step, target in enumerate(beside):
        exchange(parts.at[step], parts_in.at[step], sems, steps_req + step, target)
        parts[step + 1] = parts[step] + parts_in[step]
    mean_square = parts[steps_tp, chunks, :, :128] / D
    norm[...] = jnp.sqrt(mean_square)
    peak = jnp.max(jnp.max(parts[steps_tp, :chunks], axis=0), axis=1, keepdims=True)
    tops[0] = peak * lax.rsqrt(mean_square + eps)
    for step, target in enumerate(targets):
        exchange(tops.at[step], tops_in.at[step], sems, steps_req + steps_tp + step, target)
        tops[step + 1] = jnp.maximum(tops[step], tops_in[step])
    top[...] = tops[steps_req]


def finish(select, hidden, head_gain, vocab_weight):
    requests = select.shape[1]
    depth, words = vocab_weight.shape
    steps_req = lax.axis_size("req").bit_length() - 1
    steps_tp = lax.axis_size("tp").bit_length() - 1
    chunks = 5 if words % 80 == 0 else 1
    in_vmem = pl.BlockSpec(memory_space=pltpu.VMEM)
    small = jax.ShapeDtypeStruct((requests, 128), jnp.float32)
    norm, top = pl.pallas_call(
        functools.partial(finish_kernel, steps_req, steps_tp),
        in_specs=[in_vmem, in_vmem, in_vmem, pl.BlockSpec(memory_space=pl.ANY)],
        out_specs=[in_vmem, in_vmem],
        out_shape=[small, small],
        scratch_shapes=[
            pltpu.VMEM((chunks, words // chunks, depth), jnp.bfloat16),
            pltpu.VMEM((requests, depth), jnp.bfloat16),
            pltpu.VMEM((steps_req + 1, requests, depth), jnp.float32),
            pltpu.VMEM((steps_req, requests, depth), jnp.float32),
            pltpu.VMEM((steps_tp + 1, chunks + 1, requests, words // chunks), jnp.float32),
            pltpu.VMEM((steps_tp, chunks + 1, requests, words // chunks), jnp.float32),
            pltpu.VMEM((steps_req + 1, requests, 128), jnp.float32),
            pltpu.VMEM((steps_req, requests, 128), jnp.float32),
            pltpu.SemaphoreType.DMA((chunks,)),
            pltpu.SemaphoreType.DMA((2, 2 * steps_req + steps_tp)),
        ],
        compiler_params=pltpu.CompilerParams(
            collective_id=0, has_side_effects=True, vmem_limit_bytes=48 * 2**20
        ),
        cost_estimate=pl.CostEstimate(
            flops=2 * requests * depth * words,
            bytes_accessed=2 * depth * words,
            transcendentals=0,
        ),
    )(select, hidden, head_gain[None, :], vocab_weight.T)
    return norm[:, 0], top[:, 0]


def near_kernel(segment, found, landing, sems):
    me = lax.axis_index("req")
    last = lax.axis_size("req") - 1
    jumps = list(range(1, REACH + 1)) + [-1]

    def send(number):
        return pltpu.make_async_remote_copy(
            src_ref=segment,
            dst_ref=landing.at[number],
            send_sem=sems.at[0, number],
            recv_sem=sems.at[1, number],
            device_id={"req": me + jumps[number]},
            device_id_type=pl.DeviceIdType.MESH,
        )

    barrier = pltpu.get_barrier_semaphore()
    for jump in jumps:

        @pl.when((me - jump >= 0) & (me - jump <= last))
        def _():
            pl.semaphore_signal(
                barrier,
                inc=1,
                device_id={"req": me - jump},
                device_id_type=pl.DeviceIdType.MESH,
            )

    pl.semaphore_wait(barrier, jnp.minimum(last - me, REACH) + jnp.minimum(me, 1))
    for number, jump in enumerate(jumps):

        @pl.when((me + jump >= 0) & (me + jump <= last))
        def _():
            send(number).start()

    for number, jump in enumerate(jumps):
        came = (me - jump >= 0) & (me - jump <= last)

        @pl.when(came)
        def _():
            send(number).wait_recv()
            found[number] = landing[number]

        @pl.when(jnp.logical_not(came))
        def _():
            found[number] = jnp.zeros(found.shape[1:], jnp.int32)

    for number, jump in enumerate(jumps):

        @pl.when((me + jump >= 0) & (me + jump <= last))
        def _():
            send(number).wait_send()


def near_segments(segment):
    shape = (REACH + 1, segment.shape[0] // 128, 128)
    in_vmem = pl.BlockSpec(memory_space=pltpu.VMEM)
    return pl.pallas_call(
        near_kernel,
        in_specs=[in_vmem],
        out_specs=in_vmem,
        out_shape=jax.ShapeDtypeStruct(shape, jnp.int32),
        scratch_shapes=[
            pltpu.VMEM(shape, jnp.int32),
            pltpu.SemaphoreType.DMA((2, REACH + 1)),
        ],
        compiler_params=pltpu.CompilerParams(collective_id=2, has_side_effects=True),
    )(segment.reshape(shape[1:])).reshape(REACH + 1, -1)


def local(queries, key_value, segment, residual, out_weight, head_gain, vocab_weight):
    tok_rows = segment.shape[0]
    requests = lax.axis_size("req") // 2
    device = lax.axis_index("req")
    request_ids = jnp.arange(requests, dtype=jnp.int32)
    around = near_segments(segment)
    segments = [around[steps - 1] for steps in range(REACH, 0, -1)] + [segment]
    following = around[REACH]
    near = jnp.concatenate(segments)
    span = near.shape[0]
    at = jnp.arange(span, dtype=jnp.int32)
    real = at + (device - REACH) * tok_rows >= 0
    member = near[:, None] == request_ids[None, :]
    first = jnp.min(jnp.where(member & real[:, None], at[:, None], span), axis=0)
    start_at = jnp.sum(jnp.where(member, first[None, :], 0), axis=1)
    cosine, sine_table = rope_tables((at - start_at).astype(jnp.float32), HD)
    cosine = jnp.concatenate([cosine, cosine], axis=1)
    sine_table = jnp.concatenate([-sine_table, sine_table], axis=1)
    own_start = start_at[span - tok_rows :, None]
    if lax.axis_size("req") == 16 and lax.axis_size("tp") == 2:
        hidden, key_cache = attend_and_project(
            own_start, cosine, sine_table, queries, key_value, out_weight, residual
        )
    else:
        blocks = [from_behind(key_value, "req", steps) for steps in range(REACH, 0, -1)]
        attended, key_cache = attend(own_start, cosine, sine_table, queries, blocks + [key_value])
        hidden = project_by_weights(attended, out_weight, residual)
    after = jnp.concatenate([segment[1:], following[:1]])
    final = (device == lax.axis_size("req") - 1) & (jnp.arange(tok_rows) == tok_rows - 1)
    is_end = (segment != after) | final
    select = (is_end[:, None] & (segment[:, None] == request_ids[None, :])).astype(jnp.bfloat16)
    last_norm, top_logit = finish(select, hidden, head_gain, vocab_weight)
    return (hidden, key_cache, last_norm, top_logit)


def solution(mesh):
    placed = (
        P("req", "tp"),
        P(None, "req", "tp"),
        P("req"),
        P("req", "tp"),
        P("tp", "req"),
        P("tp"),
        P("tp", "req"),
    )
    return jax.shard_map(
        local,
        mesh=mesh,
        in_specs=placed,
        out_specs=(P("req", "tp"), P("req", "tp"), P(), P()),
        check_vma=False,
    )
```
